512 devices in a mesh: group: 32 (over z_hi, x, core), mp: 16 (over y, z_lo).
Axes of the slice: x: 4, y: 8, z: 8 (z_hi: 4, z_lo: 2; z = z_hi * 2 + z_lo), core: 2. Of those that a mesh axis runs over, the one named last changes fastest.
Arguments:
- queries: bfloat16 [640, 4096], P('group', 'mp'), may hold values from -6 to 6
- new_kv: bfloat16 [2, 640, 2048], P(None, 'group', 'mp'), may hold values from -6 to 6
- kv_pool: bfloat16 [2, 512, 128, 2048], P(None, 'group', None, 'mp'), may hold values from -6 to 6
- block_table: int32 [32, 16], P('group'), may hold values from 0 to 15, each once within a row
- lengths: int32 [32, 4], replicated, may hold values from 1 to 512, as said below
- mig_slot: int32 [32], replicated, may hold values from 0 to 3
- mig_hop: int32 [1], replicated, may hold values from 1 to 31
- handover: int32 [32], replicated, may hold values from 1 to 3
- out_weight: bfloat16 [4096, 7168], P('mp'), may hold values from -0.75 to 0.75
Outputs:
- attn_out: bfloat16 [640, 7168], P('group', 'mp')
The draws below stay inside these ranges and needn't reach their ends.
Inputs may be any that keep to these rules, and one draw needn't show every extreme that they name: `block_table`: each group's row orders its 16 cache blocks; request b owns entries b * 4 to (b + 1) * 4 - 1. `lengths`: some request holds exactly 512 tokens. Every group sends one request to group (g + mig_hop) mod 32.
All inputs are finite; a program needn't handle non-finite values.
Results may differ from the reference program's by a relative error of at most 0.013.
Values may be sent and summed in bfloat16 or wider, within the bound.
A program may use at most 64 MiB of HBM per device.

```python
import jax
import jax.numpy as jnp
from jax import lax

D = 7168
QH = 32
HD = 128
BLK = 128
MAXB = 4
STEPS = 4
SLOTS = 4
KVS = 16
REP = 2
MAXL = 512
NB = 16
GROUPS = 32
POOL = 512
ROWS = 640


def draw_kv_pool(key, part):
    key = jax.random.fold_in(key, 11)
    shape = (2, POOL, BLK, KVS * HD)
    values_drawn = jnp.clip(jax.random.normal(key, shape, jnp.float32), -6.0, 6.0)
    return values_drawn.astype(jnp.bfloat16)


def draw_queries(key, part):
    key = jax.random.fold_in(key, 12)
    shape = (ROWS, QH * HD)
    values_drawn = jnp.clip(jax.random.normal(key, shape, jnp.float32), -6.0, 6.0)
    return values_drawn.astype(jnp.bfloat16)


def draw_lengths(key, part):
    key = jax.random.fold_in(key, 13)
    key_first, key_second, key_spot = jax.random.split(key, 3)
    first_draw = jax.random.randint(key_first, (GROUPS * SLOTS,), 1, MAXL + 1)
    second_draw = jax.random.randint(key_second, (GROUPS * SLOTS,), 1, MAXL + 1)
    shorter = jnp.minimum(first_draw, second_draw)
    chosen_spot = jax.random.randint(key_spot, (), 0, GROUPS * SLOTS)
    shorter = jnp.where(jnp.arange(GROUPS * SLOTS) == chosen_spot, MAXL, shorter)
    return shorter.reshape(GROUPS, SLOTS).astype(jnp.int32)


def with_ends(array, rng, low, high):
    longest = array.shape.index(max(array.shape))
    spots = []
    for shift in (0, 1):
        where = [jax.random.randint(jax.random.fold_in(rng, axis), (), 0, length) for axis, length in enumerate(array.shape)]
        where[longest] = (where[longest] + shift) % array.shape[longest]
        spots.append(tuple(where))
    return array.at[spots[0]].set(low).at[spots[1]].set(high)


def steps_of(stream_key, extent, shards, low, top_value):
    gain = 1.0
    for position, shards_of in shards:
        draws = jax.random.uniform(jax.random.fold_in(jax.random.fold_in(stream_key, 6), position), (shards_of,), jnp.float32, low / len(shards), top_value / len(shards))
        gain = gain * jnp.repeat(jnp.exp(draws), extent[position] // shards_of).reshape((-1,) + (1,) * (len(extent) - 1 - position))
    return gain


def gaussian(rng, shape, spread, limit, shards=(), kind=jnp.bfloat16):
    result = jax.random.normal(rng, shape, jnp.float32) * spread
    if len(shards) > 0:
        result = steps_of(rng, shape, shards, -0.22, 0.18) * result
    return jnp.clip(result, min=-limit, max=limit).astype(kind)


def setup_inputs(seed: int = 0) -> dict:
    streams_of = jax.random.split(jax.random.key(seed), 10)
    return {
        "queries": draw_queries(jax.random.fold_in(streams_of[9], 71), 0),
        "new_kv": gaussian(streams_of[1], (2, ROWS, KVS * HD), 1.0, 6.0, ((1, 32), (2, 16))),
        "kv_pool": draw_kv_pool(jax.random.fold_in(streams_of[9], 71), 0),
        "block_table": jax.vmap(lambda own: jax.random.permutation(own, NB))(jax.random.split(streams_of[3], GROUPS)).reshape((GROUPS, NB)).astype(jnp.int32),
        "lengths": draw_lengths(jax.random.fold_in(streams_of[9], 71), 0),
        "mig_slot": with_ends(jax.random.randint(streams_of[5], (GROUPS,), 0, SLOTS), jax.random.fold_in(streams_of[5], 1), 0, SLOTS - 1).astype(jnp.int32),
        "mig_hop": jax.random.randint(streams_of[6], (1,), 1, GROUPS).astype(jnp.int32),
        "handover": with_ends(jax.random.randint(streams_of[7], (GROUPS,), 1, STEPS), jax.random.fold_in(streams_of[7], 1), 1, STEPS - 1).astype(jnp.int32),
        "out_weight": gaussian(streams_of[8], (QH * HD, D), (QH * HD // 64) ** -0.5, 0.75, ((0, 16),)),
    }


masked_score = -1e30


def attend(queries, keys, values, visible):
    scores = jnp.einsum("trkqd,rjkd->trkqj", queries.astype(jnp.float32), keys.astype(jnp.float32)) * (HD ** -0.5)
    scores = jnp.where(visible[:, :, None, None, :], scores, masked_score)
    maxima = jnp.max(scores, axis=-1)
    weights = jnp.exp(scores - maxima[..., None]).astype(jnp.bfloat16)
    totals = jnp.sum(weights.astype(jnp.float32), axis=-1)
    weighted = jnp.einsum("trkqj,rjkd->trkqd", weights.astype(jnp.float32), values.astype(jnp.float32))
    return maxima, totals, weighted


def reference(queries, new_kv, kv_pool, block_table, lengths, mig_slot, mig_hop, handover, out_weight):
    group_rows = STEPS * (SLOTS + 1)
    row_width = KVS * HD
    step_ids = jnp.arange(STEPS, dtype=jnp.int32)
    slot_ids = jnp.arange(SLOTS + 1, dtype=jnp.int32)
    positions = jnp.arange(MAXL, dtype=jnp.int32)

    def one_group(group_id):
        source = (group_id - mig_hop[0]) % GROUPS
        own_pool = lax.dynamic_slice_in_dim(kv_pool, group_id * NB, NB, 1)
        src_pool = lax.dynamic_slice_in_dim(kv_pool, source * NB, NB, 1)
        own_table = block_table[group_id].reshape(SLOTS, MAXB)
        src_slot = mig_slot[source]
        src_blocks = block_table[source].reshape(SLOTS, MAXB)[src_slot]
        own_cache = own_pool[:, own_table].reshape(2, SLOTS, MAXL, row_width)
        src_cache = src_pool[:, src_blocks].reshape(2, 1, MAXL, row_width)
        own_new = lax.dynamic_slice_in_dim(new_kv, group_id * group_rows, group_rows, 1).reshape(2, STEPS, SLOTS + 1, row_width)
        src_new = lax.dynamic_slice_in_dim(new_kv, source * group_rows, group_rows, 1).reshape(2, STEPS, SLOTS + 1, row_width)[:, :, src_slot]
        src_hand = handover[source]
        arrived_new = jnp.where((step_ids < src_hand)[None, :, None], src_new, own_new[:, :, SLOTS])
        cached = jnp.concatenate([own_cache, src_cache], axis=1)
        fresh_kv = jnp.concatenate([own_new[:, :, :SLOTS], arrived_new[:, :, None]], axis=2).transpose(0, 2, 1, 3)
        keys_values = jnp.concatenate([cached, fresh_kv], axis=2).reshape(2, SLOTS + 1, MAXL + STEPS, KVS, HD)
        cache_len = jnp.concatenate([lengths[group_id], lengths[source, src_slot][None]])
        cache_ok = jnp.broadcast_to((positions[None, :] < cache_len[:, None])[None], (STEPS, SLOTS + 1, MAXL))
        new_ok = jnp.broadcast_to((step_ids[None, :] <= step_ids[:, None])[:, None, :], (STEPS, SLOTS + 1, STEPS))
        visible = jnp.concatenate([cache_ok, new_ok], axis=-1)
        asked = lax.dynamic_slice_in_dim(queries, group_id * group_rows, group_rows, 0).reshape(STEPS, SLOTS + 1, KVS, REP, HD)
        maxima, totals, weighted = attend(asked, keys_values[0], keys_values[1], visible)
        context = (weighted / totals[..., None]).astype(jnp.bfloat16)
        stays = (slot_ids[None, :] < SLOTS) & ~((slot_ids[None, :] == mig_slot[group_id]) & (step_ids[:, None] >= handover[group_id]))
        arrives = (slot_ids[None, :] == SLOTS) & (step_ids[:, None] >= src_hand)
        active = stays | arrives
        context = jnp.where(active[:, :, None, None, None], context, jnp.zeros((), jnp.bfloat16)).reshape(group_rows, QH * HD)
        return jnp.dot(context, out_weight, preferred_element_type=jnp.float32).astype(jnp.bfloat16)

    output = lax.map(one_group, jnp.arange(GROUPS, dtype=jnp.int32))
    return output.reshape(ROWS, D)
```

```python
import functools

import jax
import jax.numpy as jnp
from jax import lax
from jax.experimental import pallas as pl
from jax.experimental.pallas import tpu as pltpu
from jax.sharding import PartitionSpec as P

HD = 128
MAXB = 4
STEPS = 4
SLOTS = 4
MAXL = 512
MASKED = -1e30

Z_HI = 4
XC = 8
YS = 8
PAIR = 896
WIN = 512

ORDER = (4, 3, 5, 2, 6, 1, 7, 0)

BF = jnp.bfloat16
F32 = jnp.float32


def remote(src, dst, send, recv, device):
    return pltpu.make_async_remote_copy(
        src_ref=src, dst_ref=dst, send_sem=send, recv_sem=recv,
        device_id=device, device_id_type=pl.DeviceIdType.MESH,
    )


def kernel(
    table, lengths, mig_slot, mig_hop, handover, q_ref, new_ref, kv_hbm, w_hbm, out_ref,
    qf, nf, kv, w, part, zrecv, ysend, yrecv, msg, a1, a2, st1, b0, b1, b2, st2, outf,
    kv_sem, w_sem, zs, zr, ysem, yr, a1s, a1r, a2s, a2r, b1s, b1r, b2s, b2r,
):
    g = lax.axis_index("group")
    m = lax.axis_index("mp")
    plane, spot = g // XC, g % XC
    y, zl = m // 2, m % 2

    kv_copies = [pltpu.make_async_copy(kv_hbm.at[i], kv.at[i], kv_sem.at[i]) for i in range(2)]
    for copy in kv_copies:
        copy.start()
    chunk_of = [(y + off) % YS for off in ORDER]
    w_copies = []
    for i in range(YS):
        columns = pl.ds(pl.multiple_of(chunk_of[i] * PAIR, 128), PAIR)
        w_copies.append(pltpu.make_async_copy(w_hbm.at[:, columns], w.at[i], w_sem.at[i]))
        w_copies[-1].start()

    plane_peers = [{"group": (plane + k) % Z_HI * XC + spot, "mp": m} for k in range(1, Z_HI)]
    spot_peers = [{"group": plane * XC + (spot + k) % XC, "mp": m} for k in range(1, XC)]
    pair_peer = {"group": g, "mp": y * 2 + 1 - zl}
    y_peers = [{"group": g, "mp": chunk_of[i] * 2 + zl} for i in range(YS - 1)]
    barrier = pltpu.get_barrier_semaphore()
    peers = plane_peers + spot_peers + [pair_peer] + y_peers
    for peer in peers:
        pl.semaphore_signal(barrier, inc=1, device_id=peer, device_id_type=pl.DeviceIdType.MESH)

    qf[0] = q_ref[:, :HD].astype(F32)
    qf[1] = q_ref[:, HD:].astype(F32)
    nf[...] = new_ref[...].astype(F32)
    step_rows = [pl.ds(r, STEPS, stride=SLOTS + 1) for r in range(SLOTS + 1)]

    def own_rows(r):
        return (
            jnp.concatenate([qf[0, step_rows[r], :], qf[1, step_rows[r], :]], axis=0),
            nf[0, step_rows[r], :],
            nf[1, step_rows[r], :],
        )

    q4, k4, v4 = own_rows(SLOTS)
    packed = jnp.concatenate([q4, k4, v4], axis=0).astype(BF)
    msg[...] = packed
    a1[0] = packed

    pl.semaphore_wait(barrier, len(peers))

    hop = mig_hop[0]

    def exchange(first, stage1, stage, stage2, s1, r1, s2, r2, towards):
        one = [
            remote(first, stage1.at[k], s1.at[k], r1.at[k], plane_peers[k - 1])
            for k in range(1, Z_HI)
        ]
        for copy in one:
            copy.start()
        for copy in one:
            copy.wait()
        two = []
        for k in range(XC):
            target = plane * XC + (spot + k) % XC
            owner = (target - towards + 64) % 32
            slot = (plane - owner // XC + Z_HI) % Z_HI
            if k == 0:
                stage2[0] = stage1[slot]
            else:
                stage[k] = stage1[slot]
                two.append(remote(stage.at[k], stage2.at[k], s2.at[k], r2.at[k], spot_peers[k - 1]))
                two[-1].start()
        for copy in two:
            copy.wait()
        owner = (g - towards + 64) % 32
        return stage2[(spot - owner % XC + XC) % XC]

    arrived = exchange(msg, a1, st1, a2, a1s, a1r, a2s, a2r, -hop).astype(F32)

    my_slot = mig_slot[g]
    my_hand = handover[g]
    source = (g - hop + 32) % 32
    src_hand = handover[source]

    for copy in kv_copies:
        copy.wait()

    row8 = lax.broadcasted_iota(jnp.int32, (8, 1), 0) % STEPS
    row4 = lax.broadcasted_iota(jnp.int32, (4, 1), 0)
    queries, keys_new, values_new = [], [], []
    for r in range(SLOTS):
        q, k, v = own_rows(r)
        moved = jnp.where(my_slot == r, my_hand, STEPS)
        queries.append(jnp.where(row8 >= moved, arrived[0:8], q).astype(BF))
        keys_new.append(jnp.where(row4 >= moved, arrived[8:12], k))
        values_new.append(jnp.where(row4 >= moved, arrived[12:16], v))
    keys_new = jnp.concatenate(keys_new, axis=0).astype(BF)
    values_new = jnp.concatenate(values_new, axis=0).astype(BF)

    scale = HD ** (-0.5)
    contract_last = (((1,), (1,)), ((), ()))
    lane = lax.broadcasted_iota(jnp.int32, (8, MAXL), 1)
    lane16 = lax.broadcasted_iota(jnp.int32, (8, 16), 1)
    row16 = lax.broadcasted_iota(jnp.int32, (8, 16), 0) % STEPS
    context = []
    for r in range(SLOTS):
        blocks = [table[0, r * MAXB + j] for j in range(MAXB)]
        keys = jnp.concatenate([kv[0, block] for block in blocks], axis=0)
        values = jnp.concatenate([kv[1, block] for block in blocks], axis=0)
        cached = lax.dot_general(queries[r], keys, contract_last, preferred_element_type=F32) * scale
        fresh = lax.dot_general(queries[r], keys_new, contract_last, preferred_element_type=F32) * scale
        cached = jnp.where(lane < lengths[g, r], cached, MASKED)
        fresh = jnp.where((lane16 // STEPS == r) & (lane16 % STEPS <= row16), fresh, MASKED)
        top = jnp.maximum(
            jnp.max(cached, axis=1, keepdims=True), jnp.max(fresh, axis=1, keepdims=True)
        )
        cached = jnp.exp(cached - top).astype(BF)
        fresh = jnp.exp(fresh - top).astype(BF)
        total = jnp.sum(cached.astype(F32), axis=1, keepdims=True) + jnp.sum(
            fresh.astype(F32), axis=1, keepdims=True
        )
        weighted = jnp.dot(cached, values, preferred_element_type=F32) + jnp.dot(
            fresh, values_new, preferred_element_type=F32
        )
        rows = weighted / total
        context.append(jnp.concatenate([rows[:STEPS], rows[STEPS:]], axis=1))
    context = jnp.concatenate(context, axis=0).astype(BF)

    z_copies = []
    theirs = pl.ds(pl.multiple_of((1 - zl) * (PAIR - WIN), 128), WIN)
    ours = pl.ds(pl.multiple_of(zl * (PAIR - WIN), 128), WIN)
    for i in range(YS):
        w_copies[i].wait()
        part[i] = jnp.dot(context, w[i], preferred_element_type=F32).astype(BF)
        z_copies.append(remote(part.at[i, :, theirs], zrecv.at[i], zs.at[i], zr.at[i], pair_peer))
        z_copies[-1].start()

    y_copies = []
    for i in range(YS):
        z_copies[i].wait_recv()
        both = part[i, :, ours].astype(F32) + zrecv[i].astype(F32)
        if i < YS - 1:
            ysend[i] = both.astype(BF)
            y_copies.append(remote(ysend.at[i], yrecv.at[i], ysem.at[i], yr.at[i], y_peers[i]))
            y_copies[-1].start()
    total = both
    for i in range(YS - 1):
        y_copies[i].wait_recv()
        total = total + yrecv[i].astype(F32)
    for copy in z_copies + y_copies:
        copy.wait_send()

    total = jnp.where(zl == 0, total, pltpu.roll(total, PAIR // 2, 1))

    moving = total[0:4]
    for r in range(1, SLOTS):
        moving = jnp.where(my_slot == r, total[4 * r : 4 * r + 4], moving)
    packed = jnp.concatenate([moving[:, c * 128 : c * 128 + 128] for c in range(4)], axis=0).astype(BF)
    b0[...] = packed
    b1[0] = packed
    back = exchange(b0, b1, st2, b2, b1s, b1r, b2s, b2r, hop).astype(F32)
    for c in range(4):
        for r in range(SLOTS):
            moved = jnp.where(my_slot == r, my_hand, STEPS)
            stayed = total[4 * r : 4 * r + 4, c * 128 : c * 128 + 128]
            outf[c, step_rows[r], :] = jnp.where(row4 >= moved, 0.0, stayed)
        outf[c, step_rows[SLOTS], :] = jnp.where(row4 >= src_hand, back[4 * c : 4 * c + 4], 0.0)
    wide = jnp.concatenate([outf[c] for c in range(4)], axis=1)
    out_ref[...] = wide[:, : PAIR // 2].astype(BF)


def on_device(
    queries, new_kv, kv_pool, block_table, lengths, mig_slot, mig_hop, handover, out_weight
):
    rows = STEPS * (SLOTS + 1)
    width = out_weight.shape[1]
    smem = pl.BlockSpec(memory_space=pltpu.SMEM)
    vmem = pl.BlockSpec(memory_space=pltpu.VMEM)
    hbm = pl.BlockSpec(memory_space=pltpu.HBM)
    dma = lambda n: pltpu.SemaphoreType.DMA((n,))
    tile = (16, 128)
    return pl.pallas_call(
        kernel,
        out_shape=jax.ShapeDtypeStruct((rows, PAIR // 2), BF),
        in_specs=[smem] * 5 + [vmem, vmem, hbm, hbm],
        out_specs=vmem,
        scratch_shapes=[
            pltpu.VMEM((2, rows, HD), F32),
            pltpu.VMEM((2, rows, HD), F32),
            pltpu.VMEM(kv_pool.shape, BF),
            pltpu.VMEM((YS, 2 * HD, PAIR), BF),
            pltpu.VMEM((YS, 16, PAIR), BF),
            pltpu.VMEM((YS, 16, WIN), BF),
            pltpu.VMEM((YS, 16, WIN), BF),
            pltpu.VMEM((YS, 16, WIN), BF),
            pltpu.VMEM(tile, BF),
            pltpu.VMEM((Z_HI,) + tile, BF),
            pltpu.VMEM((XC,) + tile, BF),
            pltpu.VMEM((XC,) + tile, BF),
            pltpu.VMEM(tile, BF),
            pltpu.VMEM((Z_HI,) + tile, BF),
            pltpu.VMEM((XC,) + tile, BF),
            pltpu.VMEM((XC,) + tile, BF),
            pltpu.VMEM((4, rows, 128), F32),
            dma(2), dma(YS), dma(YS), dma(YS), dma(YS), dma(YS),
            dma(Z_HI), dma(Z_HI), dma(XC), dma(XC),
            dma(Z_HI), dma(Z_HI), dma(XC), dma(XC),
        ],
        compiler_params=pltpu.CompilerParams(
            collective_id=0, has_side_effects=True, vmem_limit_bytes=32 * 1024 * 1024
        ),
        cost_estimate=pl.CostEstimate(
            flops=2 * 16 * 256 * width, bytes_accessed=5 * 1024 * 1024, transcendentals=32 * 512
        ),
    )(block_table, lengths, mig_slot, mig_hop, handover, queries, new_kv, kv_pool, out_weight)


def solution(mesh):
    in_specs = (
        P("group", "mp"),
        P(None, "group", "mp"),
        P(None, "group", None, "mp"),
        P("group", None),
        P(),
        P(),
        P(),
        P(),
        P("mp", None),
    )
    return jax.shard_map(
        on_device, mesh=mesh, in_specs=in_specs, out_specs=P("group", "mp"), check_vma=False
    )
```

```python
import functools

import jax
import jax.numpy as jnp
from jax import lax
from jax.experimental import pallas as pl
from jax.experimental.pallas import tpu as pltpu
from jax.sharding import PartitionSpec as P

HD = 128
MAXB = 4
STEPS = 4
SLOTS = 4
MAXL = 512
MASKED = -1e30

YS = 8
PAIR = 896
WIN = 512

ORDER = (4, 3, 5, 2, 6, 1, 7, 0)

BF = jnp.bfloat16
F32 = jnp.float32


def remote(src, dst, send, recv, device):
    return pltpu.make_async_remote_copy(
        src_ref=src, dst_ref=dst, send_sem=send, recv_sem=recv,
        device_id=device, device_id_type=pl.DeviceIdType.MESH,
    )


def kernel(
    hop, table_hbm, lengths_hbm, mig_slot_hbm, handover_hbm, q_hbm, new_hbm, kv_hbm, w_hbm,
    out_ref,
    table, lengths, mig_slot, handover, q_ref, new_ref, qf, nf, kv, w, part, zrecv, ysend, yrecv, msg, asked, b0, answered, outf,
    small_sem, kv_sem, w_sem, zs, zr, ysem, yr, move_sem,
):
    g = lax.axis_index("group")
    m = lax.axis_index("mp")
    y, zl = m // 2, m % 2

    small = (
        (q_hbm, q_ref), (new_hbm, new_ref), (mig_slot_hbm, mig_slot), (handover_hbm, handover),
        (table_hbm, table), (lengths_hbm, lengths),
    )
    small = [pltpu.make_async_copy(src, dst, small_sem.at[i]) for i, (src, dst) in enumerate(small)]
    for copy in small:
        copy.start()
    kv_copies = [pltpu.make_async_copy(kv_hbm.at[i], kv.at[i], kv_sem.at[i]) for i in range(2)]
    for copy in kv_copies:
        copy.start()
    chunk_of = [(y + off) % YS for off in ORDER]
    w_copies = []
    for i in range(YS):
        columns = pl.ds(pl.multiple_of(chunk_of[i] * PAIR, 128), PAIR)
        w_copies.append(pltpu.make_async_copy(w_hbm.at[:, columns], w.at[i], w_sem.at[i]))
        w_copies[-1].start()

    pair_peer = {"group": g, "mp": y * 2 + 1 - zl}
    y_peers = [{"group": g, "mp": chunk_of[i] * 2 + zl} for i in range(YS - 1)]
    barrier = pltpu.get_barrier_semaphore()
    peers = y_peers + [pair_peer] + [{"group": (g + k) % 32, "mp": m} for k in (hop, 32 - hop)]
    for peer in peers:
        pl.semaphore_signal(barrier, inc=1, device_id=peer, device_id_type=pl.DeviceIdType.MESH)

    small[0].wait()
    small[1].wait()
    qf[0] = q_ref[:, :HD].astype(F32)
    qf[1] = q_ref[:, HD:].astype(F32)
    nf[0] = new_ref[:, 0, :].astype(F32)
    nf[1] = new_ref[:, 1, :].astype(F32)
    step_rows = [pl.ds(r, STEPS, stride=SLOTS + 1) for r in range(SLOTS + 1)]

    def own_rows(r):
        return (
            jnp.concatenate([qf[0, step_rows[r], :], qf[1, step_rows[r], :]], axis=0),
            nf[0, step_rows[r], :],
            nf[1, step_rows[r], :],
        )

    q4, k4, v4 = own_rows(SLOTS)
    packed = jnp.concatenate([q4, k4, v4], axis=0).astype(BF)
    msg[...] = packed

    pl.semaphore_wait(barrier, len(peers))

    for copy in small[2:]:
        copy.wait()

    ask = remote(msg, asked, move_sem.at[0], move_sem.at[1], {"group": (g + 32 - hop) % 32, "mp": m})
    ask.start()
    ask.wait_recv()
    arrived = asked[...].astype(F32)

    my_slot = mig_slot[g]
    my_hand = handover[g]
    source = (g - hop + 32) % 32
    src_hand = handover[source]

    for copy in kv_copies:
        copy.wait()

    row8 = lax.broadcasted_iota(jnp.int32, (8, 1), 0) % STEPS
    row4 = lax.broadcasted_iota(jnp.int32, (4, 1), 0)
    queries, keys_new, values_new = [], [], []
    for r in range(SLOTS):
        q, k, v = own_rows(r)
        moved = jnp.where(my_slot == r, my_hand, STEPS)
        queries.append(jnp.where(row8 >= moved, arrived[0:8], q).astype(BF))
        keys_new.append(jnp.where(row4 >= moved, arrived[8:12], k))
        values_new.append(jnp.where(row4 >= moved, arrived[12:16], v))
    keys_new = jnp.concatenate(keys_new, axis=0).astype(BF)
    values_new = jnp.concatenate(values_new, axis=0).astype(BF)

    scale = HD ** (-0.5)
    contract_last = (((1,), (1,)), ((), ()))
    lane = lax.broadcasted_iota(jnp.int32, (8, MAXL), 1)
    lane16 = lax.broadcasted_iota(jnp.int32, (8, 16), 1)
    row16 = lax.broadcasted_iota(jnp.int32, (8, 16), 0) % STEPS
    context = []
    for r in range(SLOTS):
        blocks = [table[0, r * MAXB + j] for j in range(MAXB)]
        keys = jnp.concatenate([kv[0, block] for block in blocks], axis=0)
        values = jnp.concatenate([kv[1, block] for block in blocks], axis=0)
        cached = lax.dot_general(queries[r], keys, contract_last, preferred_element_type=F32) * scale
        fresh = lax.dot_general(queries[r], keys_new, contract_last, preferred_element_type=F32) * scale
        cached = jnp.where(lane < lengths[r, g], cached, MASKED)
        fresh = jnp.where((lane16 // STEPS == r) & (lane16 % STEPS <= row16), fresh, MASKED)
        top = jnp.maximum(
            jnp.max(cached, axis=1, keepdims=True), jnp.max(fresh, axis=1, keepdims=True)
        )
        cached = jnp.exp(cached - top).astype(BF)
        fresh = jnp.exp(fresh - top).astype(BF)
        total = jnp.sum(cached.astype(F32), axis=1, keepdims=True) + jnp.sum(
            fresh.astype(F32), axis=1, keepdims=True
        )
        weighted = jnp.dot(cached, values, preferred_element_type=F32) + jnp.dot(
            fresh, values_new, preferred_element_type=F32
        )
        rows = weighted / total
        context.append(jnp.concatenate([rows[:STEPS], rows[STEPS:]], axis=1))
    context = jnp.concatenate(context, axis=0).astype(BF)

    z_copies = []
    theirs = pl.ds(pl.multiple_of((1 - zl) * (PAIR - WIN), 128), WIN)
    ours = pl.ds(pl.multiple_of(zl * (PAIR - WIN), 128), WIN)
    for i in range(YS):
        w_copies[i].wait()
        part[i] = jnp.dot(context, w[i], preferred_element_type=F32).astype(BF)
        z_copies.append(remote(part.at[i, :, theirs], zrecv.at[i], zs.at[i], zr.at[i], pair_peer))
        z_copies[-1].start()

    y_copies = []
    for i in range(YS):
        z_copies[i].wait_recv()
        both = part[i, :, ours].astype(F32) + zrecv[i].astype(F32)
        if i < YS - 1:
            ysend[i] = both.astype(BF)
            y_copies.append(remote(ysend.at[i], yrecv.at[i], ysem.at[i], yr.at[i], y_peers[i]))
            y_copies[-1].start()
    total = both
    for i in range(YS - 1):
        y_copies[i].wait_recv()
        total = total + yrecv[i].astype(F32)
    for copy in z_copies + y_copies + [ask]:
        copy.wait_send()

    total = jnp.where(zl == 0, total, pltpu.roll(total, PAIR // 2, 1))

    moving = total[0:4]
    for r in range(1, SLOTS):
        moving = jnp.where(my_slot == r, total[4 * r : 4 * r + 4], moving)
    packed = jnp.concatenate([moving[:, c * 128 : c * 128 + 128] for c in range(4)], axis=0).astype(BF)
    b0[...] = packed
    answer = remote(b0, answered, move_sem.at[2], move_sem.at[3], {"group": (g + hop) % 32, "mp": m})
    answer.start()
    answer.wait_recv()
    back = answered[...].astype(F32)
    for c in range(4):
        for r in range(SLOTS):
            moved = jnp.where(my_slot == r, my_hand, STEPS)
            stayed = total[4 * r : 4 * r + 4, c * 128 : c * 128 + 128]
            outf[c, step_rows[r], :] = jnp.where(row4 >= moved, 0.0, stayed)
        outf[c, step_rows[SLOTS], :] = jnp.where(row4 >= src_hand, back[4 * c : 4 * c + 4], 0.0)
    wide = jnp.concatenate([outf[c] for c in range(4)], axis=1)
    answer.wait_send()
    out_ref[...] = wide[:, : PAIR // 2].astype(BF)


def on_device(
    queries, new_kv, kv_pool, block_table, lengths, mig_slot, mig_hop, handover, out_weight
):
    rows = STEPS * (SLOTS + 1)
    width = out_weight.shape[1]
    new_kv = new_kv.transpose(1, 0, 2)
    lengths = lengths.T
    vmem = pl.BlockSpec(memory_space=pltpu.VMEM)
    hbm = pl.BlockSpec(memory_space=pltpu.HBM)
    dma = lambda n: pltpu.SemaphoreType.DMA((n,))
    tile = (16, 128)
    call = lambda hop: pl.pallas_call(
        functools.partial(kernel, hop),
        out_shape=jax.ShapeDtypeStruct((rows, PAIR // 2), BF),
        in_specs=[hbm] * 8,
        out_specs=vmem,
        scratch_shapes=[
            pltpu.SMEM(block_table.shape, jnp.int32),
            pltpu.SMEM(lengths.shape, jnp.int32),
            pltpu.SMEM(mig_slot.shape, jnp.int32),
            pltpu.SMEM(handover.shape, jnp.int32),
            pltpu.VMEM(queries.shape, BF),
            pltpu.VMEM(new_kv.shape, BF),
            pltpu.VMEM((2, rows, HD), F32),
            pltpu.VMEM((2, rows, HD), F32),
            pltpu.VMEM(kv_pool.shape, BF),
            pltpu.VMEM((YS, 2 * HD, PAIR), BF),
            pltpu.VMEM((YS, 16, PAIR), BF),
            pltpu.VMEM((YS, 16, WIN), BF),
            pltpu.VMEM((YS, 16, WIN), BF),
            pltpu.VMEM((YS, 16, WIN), BF),
            pltpu.VMEM(tile, BF),
            pltpu.VMEM(tile, BF),
            pltpu.VMEM(tile, BF),
            pltpu.VMEM(tile, BF),
            pltpu.VMEM((4, rows, 128), F32),
            dma(6), dma(2), dma(YS), dma(YS), dma(YS), dma(YS), dma(YS),
            dma(4),
        ],
        compiler_params=pltpu.CompilerParams(
            collective_id=hop, has_side_effects=True, vmem_limit_bytes=60 * 1024 * 1024
        ),
        cost_estimate=pl.CostEstimate(
            flops=2 * 16 * 256 * width, bytes_accessed=5 * 1024 * 1024, transcendentals=32 * 512
        ),
    )
    return lax.switch(
        mig_hop[0] - 1, [call(hop) for hop in range(1, 32)],
        block_table, lengths, mig_slot, handover, queries, new_kv, kv_pool, out_weight,
    )


def solution(mesh):
    in_specs = (
        P("group", "mp"),
        P(None, "group", "mp"),
        P(None, "group", None, "mp"),
        P("group", None),
        P(),
        P(),
        P(),
        P(),
        P("mp", None),
    )
    return jax.shard_map(
        on_device, mesh=mesh, in_specs=in_specs, out_specs=P("group", "mp"), check_vma=False
    )
```

```python
import functools

import jax
import jax.numpy as jnp
from jax import lax
from jax.experimental import pallas as pl
from jax.experimental.pallas import tpu as pltpu
from jax.sharding import PartitionSpec as P

HD = 128
MAXB = 4
STEPS = 4
SLOTS = 4
MAXL = 512
GROUPS = 32
MASKED = -1e30

YS = 8
PAIR = 896
WIN = 512

ORDER = (4, 3, 5, 2, 6, 1, 7, 0)

BF = jnp.bfloat16
F32 = jnp.float32


def remote(src, dst, send, recv, device):
    return pltpu.make_async_remote_copy(
        src_ref=src, dst_ref=dst, send_sem=send, recv_sem=recv,
        device_id=device, device_id_type=pl.DeviceIdType.MESH,
    )


def attend(queries, keys, values, length, keys_new, values_new, new_ok):
    contract_last = (((1,), (1,)), ((), ()))
    scale = HD ** (-0.5)
    lane = lax.broadcasted_iota(jnp.int32, (8, MAXL), 1)
    cached = lax.dot_general(queries, keys, contract_last, preferred_element_type=F32) * scale
    fresh = lax.dot_general(queries, keys_new, contract_last, preferred_element_type=F32) * scale
    cached = jnp.where(lane < length, cached, MASKED)
    fresh = jnp.where(new_ok, fresh, MASKED)
    top = jnp.maximum(
        jnp.max(cached, axis=1, keepdims=True), jnp.max(fresh, axis=1, keepdims=True)
    )
    cached = jnp.exp(cached - top).astype(BF)
    fresh = jnp.exp(fresh - top).astype(BF)
    total = jnp.sum(cached.astype(F32), axis=1, keepdims=True) + jnp.sum(
        fresh.astype(F32), axis=1, keepdims=True
    )
    weighted = jnp.dot(cached, values, preferred_element_type=F32) + jnp.dot(
        fresh, values_new, preferred_element_type=F32
    )
    return weighted / total


def kernel(
    hop, table_hbm, lengths_hbm, mig_slot_hbm, handover_hbm, q_hbm, new_hbm, kv_hbm, w_hbm,
    out_ref,
    table, lengths, mig_slot, handover, q_ref, new_ref, qf, nf, kv, w, part, zrecv, ysend, yrecv,
    msg, asked, ctx_out, ctx_in, msend, mrecv, outf,
    small_sem, kv_sem, w_sem, zs, zr, ysem, yr, ms, mr, move_sem,
):
    g = lax.axis_index("group")
    m = lax.axis_index("mp")
    y, zl = m // 2, m % 2
    chunk_of = [(y + off) % YS for off in ORDER]
    source = (g + GROUPS - hop) % GROUPS
    target = (g + hop) % GROUPS

    same_peers = [{"group": g, "mp": chunk_of[i] * 2 + zl} for i in range(YS - 1)]
    other_peers = [{"group": g, "mp": chunk_of[i] * 2 + 1 - zl} for i in range(YS)]
    barrier = pltpu.get_barrier_semaphore()
    peers = [{"group": source, "mp": m}, {"group": target, "mp": m}]
    for i in range(YS):
        peers += [other_peers[i]] + same_peers[i : i + 1]
    for peer in peers:
        pl.semaphore_signal(barrier, inc=1, device_id=peer, device_id_type=pl.DeviceIdType.MESH)

    small = (
        (q_hbm, q_ref), (new_hbm, new_ref), (mig_slot_hbm, mig_slot), (handover_hbm, handover),
        (table_hbm, table), (lengths_hbm, lengths),
    )
    small = [pltpu.make_async_copy(src, dst, small_sem.at[i]) for i, (src, dst) in enumerate(small)]
    kv_copies = [pltpu.make_async_copy(kv_hbm.at[i], kv.at[i], kv_sem.at[i]) for i in range(2)]
    for copy in small + kv_copies:
        copy.start()
    w_copies = []
    for i in range(YS):
        columns = pl.ds(pl.multiple_of(chunk_of[i] * PAIR, 128), PAIR)
        w_copies.append(pltpu.make_async_copy(w_hbm.at[:, columns], w.at[i], w_sem.at[i]))
        w_copies[-1].start()

    small[0].wait()
    small[1].wait()
    qf[0] = q_ref[:, :HD].astype(F32)
    qf[1] = q_ref[:, HD:].astype(F32)
    nf[0] = new_ref[:, 0, :].astype(F32)
    nf[1] = new_ref[:, 1, :].astype(F32)
    step_rows = [pl.ds(r, STEPS, stride=SLOTS + 1) for r in range(SLOTS + 1)]

    def own_rows(r):
        return (
            jnp.concatenate([qf[0, step_rows[r], :], qf[1, step_rows[r], :]], axis=0),
            nf[0, step_rows[r], :],
            nf[1, step_rows[r], :],
        )

    msg[...] = jnp.concatenate(own_rows(SLOTS), axis=0).astype(BF)
    own = [own_rows(r) for r in range(SLOTS)]
    keys_new = jnp.concatenate([k for _, k, _ in own], axis=0).astype(BF)
    values_new = jnp.concatenate([v for _, _, v in own], axis=0).astype(BF)

    for copy in small[2:] + kv_copies:
        copy.wait()

    lane16 = lax.broadcasted_iota(jnp.int32, (8, 16), 1)
    row16 = lax.broadcasted_iota(jnp.int32, (8, 16), 0) % STEPS
    context = []
    for r in range(SLOTS):
        blocks = [table[0, r * MAXB + j] for j in range(MAXB)]
        rows = attend(
            own[r][0].astype(BF),
            jnp.concatenate([kv[0, block] for block in blocks], axis=0),
            jnp.concatenate([kv[1, block] for block in blocks], axis=0),
            lengths[r, g],
            keys_new,
            values_new,
            (lane16 // STEPS == r) & (lane16 % STEPS <= row16),
        )
        context.append(jnp.concatenate([rows[:STEPS], rows[STEPS:]], axis=1))
    context = jnp.concatenate(context, axis=0).astype(BF)

    pl.semaphore_wait(barrier, len(peers))

    ask = remote(msg, asked, move_sem.at[0], move_sem.at[1], {"group": source, "mp": m})
    ask.start()
    z_copies = []
    theirs = pl.ds(pl.multiple_of((1 - zl) * (PAIR - WIN), 128), WIN)
    ours = pl.ds(pl.multiple_of(zl * (PAIR - WIN), 128), WIN)
    for i in range(YS):
        w_copies[i].wait()
        part[i] = jnp.dot(context, w[i], preferred_element_type=F32).astype(BF)
        z_copies.append(remote(part.at[i, :, theirs], zrecv.at[i], zs.at[i], zr.at[i], other_peers[YS - 1]))
        z_copies[-1].start()

    my_slot = mig_slot[g]
    my_hand = handover[g]
    row4 = lax.broadcasted_iota(jnp.int32, (STEPS, 1), 0)

    def of_slot(parts):
        rows = parts[0]
        for r in range(1, SLOTS):
            rows = jnp.where(my_slot == r, parts[r], rows)
        return rows

    none = jnp.zeros((16 - STEPS, HD), F32)
    keys_own = of_slot([k for _, k, _ in own])
    values_own = of_slot([v for _, _, v in own])
    blocks = [table[0, my_slot * MAXB + j] for j in range(MAXB)]
    ask.wait_recv()
    arrived = asked[...].astype(F32)
    rows = attend(
        arrived[:8].astype(BF),
        jnp.concatenate([kv[0, block] for block in blocks], axis=0),
        jnp.concatenate([kv[1, block] for block in blocks], axis=0),
        lengths[my_slot, g],
        jnp.concatenate([jnp.where(row4 >= my_hand, arrived[8:12], keys_own), none], axis=0).astype(BF),
        jnp.concatenate([jnp.where(row4 >= my_hand, arrived[12:], values_own), none], axis=0).astype(BF),
        lane16 <= row16,
    )
    rows = jnp.concatenate([rows[:STEPS], rows[STEPS:]], axis=1)
    ctx_out[...] = jnp.concatenate([rows] * 4, axis=0).astype(BF)
    give = remote(ctx_out, ctx_in, move_sem.at[2], move_sem.at[3], {"group": target, "mp": m})
    give.start()

    y_copies = []
    for i in range(YS):
        z_copies[i].wait_recv()
        both = part[i, :, ours].astype(F32) + zrecv[i].astype(F32)
        if i < YS - 1:
            ysend[i] = both.astype(BF)
            y_copies.append(remote(ysend.at[i], yrecv.at[i], ysem.at[i], yr.at[i], same_peers[i]))
            y_copies[-1].start()

    give.wait_recv()
    rows = ctx_in[...]
    tile_of = lax.broadcasted_iota(jnp.int32, (16, 128), 0) // STEPS

    def packed(product, first):
        tiles = [product[:, (first + c) * 128 : (first + c + 1) * 128] for c in range(4)]
        result = tiles[0]
        for c in range(1, 4):
            result = jnp.where(tile_of == c, tiles[c], result)
        return result

    m_copies = []
    for i in range(YS):
        product = jnp.dot(rows, w[i], preferred_element_type=F32)
        low, high = packed(product, 0), packed(product, 3)
        same, other = jnp.where(zl == 0, low, high), jnp.where(zl == 0, high, low)
        for k, (rows_of, peers_of) in enumerate(((other, other_peers), (same, same_peers))):
            if i < len(peers_of):
                n = 2 * i + k
                msend[n] = rows_of.astype(BF)
                m_copies.append(remote(msend.at[n], mrecv.at[n], ms.at[n], mr.at[n], peers_of[i]))
                m_copies[-1].start()
    total = both
    for i in range(YS - 1):
        y_copies[i].wait_recv()
        total = total + yrecv[i].astype(F32)
    total = jnp.where(zl == 0, total, pltpu.roll(total, PAIR // 2, 1))
    for c in range(4):
        for r in range(SLOTS):
            moved = jnp.where(my_slot == r, my_hand, STEPS)
            stayed = total[4 * r : 4 * r + 4, c * 128 : c * 128 + 128]
            outf[c, step_rows[r], :] = jnp.where(row4 >= moved, 0.0, stayed)

    for copy in z_copies + y_copies + [ask, give] + m_copies:
        copy.wait_send()
    for n in range(2 * YS - 1):
        m_copies[n].wait_recv()
        same = same + mrecv[n].astype(F32)
    same = jnp.concatenate([same[4 * c : 4 * c + 4] for c in range(4)], axis=1)
    same = jnp.where(zl == 0, same, pltpu.roll(same, PAIR // 2, 1))
    for c in range(4):
        outf[c, step_rows[SLOTS], :] = jnp.where(
            row4 >= handover[source], same[:, c * 128 : c * 128 + 128], 0.0
        )
    wide = jnp.concatenate([outf[c] for c in range(4)], axis=1)
    out_ref[...] = wide[:, : PAIR // 2].astype(BF)


def on_device(
    queries, new_kv, kv_pool, block_table, lengths, mig_slot, mig_hop, handover, out_weight
):
    rows = STEPS * (SLOTS + 1)
    width = out_weight.shape[1]
    new_kv = new_kv.transpose(1, 0, 2)
    lengths = lengths.T
    vmem = pl.BlockSpec(memory_space=pltpu.VMEM)
    hbm = pl.BlockSpec(memory_space=pltpu.HBM)
    dma = lambda n: pltpu.SemaphoreType.DMA((n,))
    tile = (16, 128)
    call = lambda hop: pl.pallas_call(
        functools.partial(kernel, hop),
        out_shape=jax.ShapeDtypeStruct((rows, PAIR // 2), BF),
        in_specs=[hbm] * 8,
        out_specs=vmem,
        scratch_shapes=[
            pltpu.SMEM(block_table.shape, jnp.int32),
            pltpu.SMEM(lengths.shape, jnp.int32),
            pltpu.SMEM(mig_slot.shape, jnp.int32),
            pltpu.SMEM(handover.shape, jnp.int32),
            pltpu.VMEM(queries.shape, BF),
            pltpu.VMEM(new_kv.shape, BF),
            pltpu.VMEM((2, rows, HD), F32),
            pltpu.VMEM((2, rows, HD), F32),
            pltpu.VMEM(kv_pool.shape, BF),
            pltpu.VMEM((YS, 2 * HD, PAIR), BF),
            pltpu.VMEM((YS, 16, PAIR), BF),
            pltpu.VMEM((YS, 16, WIN), BF),
            pltpu.VMEM((YS, 16, WIN), BF),
            pltpu.VMEM((YS, 16, WIN), BF),
            pltpu.VMEM(tile, BF),
            pltpu.VMEM(tile, BF),
            pltpu.VMEM((16, 2 * HD), BF),
            pltpu.VMEM((16, 2 * HD), BF),
            pltpu.VMEM((2 * YS,) + tile, BF),
            pltpu.VMEM((2 * YS,) + tile, BF),
            pltpu.VMEM((4, rows, 128), F32),
            dma(6), dma(2), dma(YS), dma(YS), dma(YS), dma(YS), dma(YS), dma(2 * YS), dma(2 * YS), dma(4),
        ],
        compiler_params=pltpu.CompilerParams(
            collective_id=hop, has_side_effects=True, vmem_limit_bytes=60 * 1024 * 1024
        ),
        cost_estimate=pl.CostEstimate(
            flops=2 * 16 * 256 * width, bytes_accessed=5 * 1024 * 1024, transcendentals=32 * 512
        ),
    )
    return lax.switch(
        mig_hop[0] - 1, [call(hop) for hop in range(1, GROUPS)],
        block_table, lengths, mig_slot, handover, queries, new_kv, kv_pool, out_weight,
    )


def solution(mesh):
    in_specs = (
        P("group", "mp"),
        P(None, "group", "mp"),
        P(None, "group", None, "mp"),
        P("group", None),
        P(),
        P(),
        P(),
        P(),
        P("mp", None),
    )
    return jax.shard_map(
        on_device, mesh=mesh, in_specs=in_specs, out_specs=P("group", "mp"), check_vma=False
    )
```

```python
import functools

import jax
import jax.numpy as jnp
from jax import lax
from jax.experimental import pallas as pl
from jax.experimental.pallas import tpu as pltpu
from jax.sharding import PartitionSpec as P

HD = 128
MAXB = 4
STEPS = 4
SLOTS = 4
MAXL = 512
GROUPS = 32
MASKED = -1e30

YS = 8
PAIR = 896
WIN = 512

BF = jnp.bfloat16
F32 = jnp.float32


def remote(src, dst, send, recv, device):
    return pltpu.make_async_remote_copy(
        src_ref=src, dst_ref=dst, send_sem=send, recv_sem=recv,
        device_id=device, device_id_type=pl.DeviceIdType.MESH,
    )


def attend(queries, keys, values, length, keys_new, values_new, new_ok):
    contract_last = (((1,), (1,)), ((), ()))
    scale = HD ** (-0.5)
    lane = lax.broadcasted_iota(jnp.int32, (8, MAXL), 1)
    cached = lax.dot_general(queries, keys, contract_last, preferred_element_type=F32) * scale
    fresh = lax.dot_general(queries, keys_new, contract_last, preferred_element_type=F32) * scale
    cached = jnp.where(lane < length, cached, MASKED)
    fresh = jnp.where(new_ok, fresh, MASKED)
    top = jnp.maximum(
        jnp.max(cached, axis=1, keepdims=True), jnp.max(fresh, axis=1, keepdims=True)
    )
    cached = jnp.exp(cached - top).astype(BF)
    fresh = jnp.exp(fresh - top).astype(BF)
    total = jnp.sum(cached.astype(F32), axis=1, keepdims=True) + jnp.sum(
        fresh.astype(F32), axis=1, keepdims=True
    )
    weighted = jnp.dot(cached, values, preferred_element_type=F32) + jnp.dot(
        fresh, values_new, preferred_element_type=F32
    )
    return weighted / total


def kernel(
    hop, table_hbm, lengths_hbm, mig_slot_hbm, handover_hbm, q_hbm, new_hbm, kv_hbm, w_hbm,
    out_ref,
    table, lengths, mig_slot, handover, q_ref, new_ref, qf, nf, kv, w, part, zrecv, ysend, yrecv,
    msg, asked, ctx_out, ctx_in, msend, mrecv, outf,
    small_sem, kv_sem, w_sem, zs, zr, ysem, yr, ms, mr, move_sem,
):
    g = lax.axis_index("group")
    m = lax.axis_index("mp")
    y, zl = m // 2, m % 2

    def chunk_of(i):
        return (y + YS // 2 + (i + 1) // 2 * (1 - 2 * (i % 2))) % YS

    source = (g + GROUPS - hop) % GROUPS
    target = (g + hop) % GROUPS

    def same_peer(i):
        return {"group": g, "mp": chunk_of(i) * 2 + zl}

    def other_peer(i):
        return {"group": g, "mp": chunk_of(i) * 2 + 1 - zl}

    barrier = pltpu.get_barrier_semaphore()
    peers = [{"group": source, "mp": m}, {"group": target, "mp": m}]
    for i in range(YS):
        peers += [other_peer(i)] + [same_peer(i)] * (i < YS - 1)
    for peer in peers:
        pl.semaphore_signal(barrier, inc=1, device_id=peer, device_id_type=pl.DeviceIdType.MESH)

    small = (
        (q_hbm, q_ref), (new_hbm, new_ref), (mig_slot_hbm, mig_slot), (handover_hbm, handover),
        (table_hbm, table), (lengths_hbm, lengths),
    )
    small = [pltpu.make_async_copy(src, dst, small_sem.at[i]) for i, (src, dst) in enumerate(small)]
    kv_copies = [pltpu.make_async_copy(kv_hbm.at[i], kv.at[i], kv_sem.at[i]) for i in range(2)]
    for copy in small + kv_copies:
        copy.start()

    def w_copy(i):
        columns = pl.ds(pl.multiple_of(chunk_of(i) * PAIR, 128), PAIR)
        return pltpu.make_async_copy(w_hbm.at[:, columns], w.at[i], w_sem.at[i])

    def each(count, body):
        lax.fori_loop(0, count, lambda i, carry: body(i) or carry, 0)

    each(YS, lambda i: w_copy(i).start())

    small[0].wait()
    small[1].wait()
    qf[0] = q_ref[:, :HD].astype(F32)
    qf[1] = q_ref[:, HD:].astype(F32)
    nf[0] = new_ref[:, 0, :].astype(F32)
    nf[1] = new_ref[:, 1, :].astype(F32)
    step_rows = [pl.ds(r, STEPS, stride=SLOTS + 1) for r in range(SLOTS + 1)]

    def own_rows(r):
        return (
            jnp.concatenate([qf[0, step_rows[r], :], qf[1, step_rows[r], :]], axis=0),
            nf[0, step_rows[r], :],
            nf[1, step_rows[r], :],
        )

    msg[...] = jnp.concatenate(own_rows(SLOTS), axis=0).astype(BF)
    own = [own_rows(r) for r in range(SLOTS)]
    keys_new = jnp.concatenate([k for _, k, _ in own], axis=0).astype(BF)
    values_new = jnp.concatenate([v for _, _, v in own], axis=0).astype(BF)

    for copy in small[2:] + kv_copies:
        copy.wait()

    lane16 = lax.broadcasted_iota(jnp.int32, (8, 16), 1)
    row16 = lax.broadcasted_iota(jnp.int32, (8, 16), 0) % STEPS
    context = []
    for r in range(SLOTS):
        blocks = [table[0, r * MAXB + j] for j in range(MAXB)]
        rows = attend(
            own[r][0].astype(BF),
            jnp.concatenate([kv[0, block] for block in blocks], axis=0),
            jnp.concatenate([kv[1, block] for block in blocks], axis=0),
            lengths[r, g],
            keys_new,
            values_new,
            (lane16 // STEPS == r) & (lane16 % STEPS <= row16),
        )
        context.append(jnp.concatenate([rows[:STEPS], rows[STEPS:]], axis=1))
    context = jnp.concatenate(context, axis=0).astype(BF)

    pl.semaphore_wait(barrier, len(peers))

    ask = remote(msg, asked, move_sem.at[0], move_sem.at[1], {"group": source, "mp": m})
    ask.start()
    theirs = pl.ds(pl.multiple_of((1 - zl) * (PAIR - WIN), 128), WIN)
    ours = pl.ds(pl.multiple_of(zl * (PAIR - WIN), 128), WIN)

    def z_copy(i):
        return remote(part.at[i, :, theirs], zrecv.at[i], zs.at[i], zr.at[i], other_peer(YS - 1))

    def project(i):
        w_copy(i).wait()
        part[i] = jnp.dot(context, w[i], preferred_element_type=F32).astype(BF)
        z_copy(i).start()

    each(YS, project)

    my_slot = mig_slot[g]
    my_hand = handover[g]
    row4 = lax.broadcasted_iota(jnp.int32, (STEPS, 1), 0)

    def of_slot(parts):
        rows = parts[0]
        for r in range(1, SLOTS):
            rows = jnp.where(my_slot == r, parts[r], rows)
        return rows

    none = jnp.zeros((16 - STEPS, HD), F32)
    keys_own = of_slot([k for _, k, _ in own])
    values_own = of_slot([v for _, _, v in own])
    blocks = [table[0, my_slot * MAXB + j] for j in range(MAXB)]
    ask.wait_recv()
    arrived = asked[...].astype(F32)
    rows = attend(
        arrived[:8].astype(BF),
        jnp.concatenate([kv[0, block] for block in blocks], axis=0),
        jnp.concatenate([kv[1, block] for block in blocks], axis=0),
        lengths[my_slot, g],
        jnp.concatenate([jnp.where(row4 >= my_hand, arrived[8:12], keys_own), none], axis=0).astype(BF),
        jnp.concatenate([jnp.where(row4 >= my_hand, arrived[12:], values_own), none], axis=0).astype(BF),
        lane16 <= row16,
    )
    rows = jnp.concatenate([rows[:STEPS], rows[STEPS:]], axis=1)
    ctx_out[...] = jnp.concatenate([rows] * 4, axis=0).astype(BF)
    give = remote(ctx_out, ctx_in, move_sem.at[2], move_sem.at[3], {"group": target, "mp": m})
    give.start()

    def y_copy(i):
        return remote(ysend.at[i], yrecv.at[i], ysem.at[i], yr.at[i], same_peer(i))

    def both(i):
        z_copy(i).wait_recv()
        return part[i, :, ours].astype(F32) + zrecv[i].astype(F32)

    def pair_sum(i):
        ysend[i] = both(i).astype(BF)
        y_copy(i).start()

    each(YS - 1, pair_sum)

    give.wait_recv()
    rows = ctx_in[...]
    tile_of = lax.broadcasted_iota(jnp.int32, (16, 128), 0) // STEPS

    def packed(product, first):
        tiles = [product[:, (first + c) * 128 : (first + c + 1) * 128] for c in range(4)]
        result = tiles[0]
        for c in range(1, 4):
            result = jnp.where(tile_of == c, tiles[c], result)
        return result

    def m_copy(i, k):
        n = 2 * i + k
        return remote(
            msend.at[n], mrecv.at[n], ms.at[n], mr.at[n], same_peer(i) if k else other_peer(i)
        )

    def project_arrived(i):
        product = jnp.dot(rows, w[i], preferred_element_type=F32)
        low, high = packed(product, 0), packed(product, 3)
        msend[2 * i] = jnp.where(zl == 0, high, low).astype(BF)
        m_copy(i, 0).start()
        return jnp.where(zl == 0, low, high)

    def send_both(i):
        msend[2 * i + 1] = project_arrived(i).astype(BF)
        m_copy(i, 1).start()

    each(YS - 1, send_both)
    same = project_arrived(YS - 1)

    def add_y(i, total):
        y_copy(i).wait_recv()
        return total + yrecv[i].astype(F32)

    total = lax.fori_loop(0, YS - 1, add_y, both(YS - 1))
    total = jnp.where(zl == 0, total, pltpu.roll(total, PAIR // 2, 1))
    for c in range(4):
        for r in range(SLOTS):
            moved = jnp.where(my_slot == r, my_hand, STEPS)
            stayed = total[4 * r : 4 * r + 4, c * 128 : c * 128 + 128]
            outf[c, step_rows[r], :] = jnp.where(row4 >= moved, 0.0, stayed)

    ask.wait_send()
    give.wait_send()

    def sent(i):
        z_copy(i).wait_send()
        y_copy(i).wait_send()
        m_copy(i, 0).wait_send()
        m_copy(i, 1).wait_send()

    each(YS - 1, sent)
    z_copy(YS - 1).wait_send()
    m_copy(YS - 1, 0).wait_send()

    def add_m(i, total):
        m_copy(i, 0).wait_recv()
        m_copy(i, 1).wait_recv()
        return total + mrecv[2 * i].astype(F32) + mrecv[2 * i + 1].astype(F32)

    same = lax.fori_loop(0, YS - 1, add_m, same)
    m_copy(YS - 1, 0).wait_recv()
    same = same + mrecv[2 * YS - 2].astype(F32)
    same = jnp.concatenate([same[4 * c : 4 * c + 4] for c in range(4)], axis=1)
    same = jnp.where(zl == 0, same, pltpu.roll(same, PAIR // 2, 1))
    for c in range(4):
        outf[c, step_rows[SLOTS], :] = jnp.where(
            row4 >= handover[source], same[:, c * 128 : c * 128 + 128], 0.0
        )
    wide = jnp.concatenate([outf[c] for c in range(4)], axis=1)
    out_ref[...] = wide[:, : PAIR // 2].astype(BF)


def on_device(
    queries, new_kv, kv_pool, block_table, lengths, mig_slot, mig_hop, handover, out_weight
):
    rows = STEPS * (SLOTS + 1)
    width = out_weight.shape[1]
    new_kv = new_kv.transpose(1, 0, 2)
    lengths = lengths.T
    vmem = pl.BlockSpec(memory_space=pltpu.VMEM)
    hbm = pl.BlockSpec(memory_space=pltpu.HBM)
    dma = lambda n: pltpu.SemaphoreType.DMA((n,))
    tile = (16, 128)
    call = lambda hop: pl.pallas_call(
        functools.partial(kernel, hop),
        out_shape=jax.ShapeDtypeStruct((rows, PAIR // 2), BF),
        in_specs=[hbm] * 8,
        out_specs=vmem,
        scratch_shapes=[
            pltpu.SMEM(block_table.shape, jnp.int32),
            pltpu.SMEM(lengths.shape, jnp.int32),
            pltpu.SMEM(mig_slot.shape, jnp.int32),
            pltpu.SMEM(handover.shape, jnp.int32),
            pltpu.VMEM(queries.shape, BF),
            pltpu.VMEM(new_kv.shape, BF),
            pltpu.VMEM((2, rows, HD), F32),
            pltpu.VMEM((2, rows, HD), F32),
            pltpu.VMEM(kv_pool.shape, BF),
            pltpu.VMEM((YS, 2 * HD, PAIR), BF),
            pltpu.VMEM((YS, 16, PAIR), BF),
            pltpu.VMEM((YS, 16, WIN), BF),
            pltpu.VMEM((YS, 16, WIN), BF),
            pltpu.VMEM((YS, 16, WIN), BF),
            pltpu.VMEM(tile, BF),
            pltpu.VMEM(tile, BF),
            pltpu.VMEM((16, 2 * HD), BF),
            pltpu.VMEM((16, 2 * HD), BF),
            pltpu.VMEM((2 * YS,) + tile, BF),
            pltpu.VMEM((2 * YS,) + tile, BF),
            pltpu.VMEM((4, rows, 128), F32),
            dma(6), dma(2), dma(YS), dma(YS), dma(YS), dma(YS), dma(YS), dma(2 * YS), dma(2 * YS), dma(4),
        ],
        compiler_params=pltpu.CompilerParams(
            collective_id=hop, has_side_effects=True, vmem_limit_bytes=60 * 1024 * 1024
        ),
        cost_estimate=pl.CostEstimate(
            flops=2 * 16 * 256 * width, bytes_accessed=5 * 1024 * 1024, transcendentals=32 * 512
        ),
    )
    return lax.switch(
        mig_hop[0] - 1, [call(hop) for hop in range(1, GROUPS)],
        block_table, lengths, mig_slot, handover, queries, new_kv, kv_pool, out_weight,
    )


def solution(mesh):
    in_specs = (
        P("group", "mp"),
        P(None, "group", "mp"),
        P(None, "group", None, "mp"),
        P("group", None),
        P(),
        P(),
        P(),
        P(),
        P("mp", None),
    )
    return jax.shard_map(
        on_device, mesh=mesh, in_specs=in_specs, out_specs=P("group", "mp"), check_vma=False
    )
```

```python
import functools

import jax
import jax.numpy as jnp
from jax import lax
from jax.experimental import pallas as pl
from jax.experimental.pallas import tpu as pltpu
from jax.sharding import PartitionSpec as P

HD = 128
MAXB = 4
STEPS = 4
SLOTS = 4
MAXL = 512
GROUPS = 32
MASKED = -1e30

YS = 8
PAIR = 896
WIN = 512

BF = jnp.bfloat16
F32 = jnp.float32


def remote(src, dst, send, recv, device):
    return pltpu.make_async_remote_copy(
        src_ref=src, dst_ref=dst, send_sem=send, recv_sem=recv,
        device_id=device, device_id_type=pl.DeviceIdType.MESH,
    )


def attend(queries, keys, values, length, keys_new, values_new, new_ok):
    contract_last = (((1,), (1,)), ((), ()))
    scale = HD ** (-0.5)
    lane = lax.broadcasted_iota(jnp.int32, (8, MAXL), 1)
    cached = lax.dot_general(queries, keys, contract_last, preferred_element_type=F32) * scale
    fresh = lax.dot_general(queries, keys_new, contract_last, preferred_element_type=F32) * scale
    cached = jnp.where(lane < length, cached, MASKED)
    fresh = jnp.where(new_ok, fresh, MASKED)
    top = jnp.maximum(
        jnp.max(cached, axis=1, keepdims=True), jnp.max(fresh, axis=1, keepdims=True)
    )
    cached = jnp.exp(cached - top).astype(BF)
    fresh = jnp.exp(fresh - top).astype(BF)
    total = jnp.sum(cached.astype(F32), axis=1, keepdims=True) + jnp.sum(
        fresh.astype(F32), axis=1, keepdims=True
    )
    weighted = jnp.dot(cached, values, preferred_element_type=F32) + jnp.dot(
        fresh, values_new, preferred_element_type=F32
    )
    return weighted / total


def kernel(
    hop, table_hbm, lengths_hbm, mig_slot_hbm, handover_hbm, q_hbm, new_hbm, kv_hbm, w_hbm,
    out_ref,
    table, lengths, mig_slot, handover, q_ref, new_ref, qf, nf, kv, w, part, zrecv, ysend, yrecv,
    msg, asked, ctx_out, ctx_in, msend, mrecv, outf,
    small_sem, kv_sem, w_sem, zs, zr, ysem, yr, ms, mr, move_sem,
):
    g = lax.axis_index("group")
    m = lax.axis_index("mp")
    y, zl = m // 2, m % 2

    def chunk_of(i):
        return (y + YS // 2 + (i + 1) // 2 * (1 - 2 * (i % 2))) % YS

    source = (g + GROUPS - hop) % GROUPS
    target = (g + hop) % GROUPS

    def same_peer(i):
        return {"group": g, "mp": chunk_of(i) * 2 + zl}

    def other_peer(i):
        return {"group": g, "mp": chunk_of(i) * 2 + 1 - zl}

    barrier = pltpu.get_barrier_semaphore()
    peers = [{"group": source, "mp": m}, {"group": target, "mp": m}]
    for i in range(YS):
        peers += [other_peer(i)] + [same_peer(i)] * (i < YS - 1)
    for peer in peers:
        pl.semaphore_signal(barrier, inc=1, device_id=peer, device_id_type=pl.DeviceIdType.MESH)

    small = (
        (q_hbm, q_ref), (new_hbm, new_ref), (mig_slot_hbm, mig_slot), (handover_hbm, handover),
        (table_hbm, table), (lengths_hbm, lengths),
    )
    small = [pltpu.make_async_copy(src, dst, small_sem.at[i]) for i, (src, dst) in enumerate(small)]
    kv_copies = [pltpu.make_async_copy(kv_hbm.at[i], kv.at[i], kv_sem.at[i]) for i in range(2)]
    for copy in small + kv_copies:
        copy.start()

    def w_copy(i):
        columns = pl.ds(pl.multiple_of(chunk_of(i) * PAIR, 128), PAIR)
        return pltpu.make_async_copy(w_hbm.at[:, columns], w.at[i], w_sem.at[i])

    def each(count, body):
        lax.fori_loop(0, count, lambda i, carry: body(i) or carry, 0)

    each(YS, lambda i: w_copy(i).start())

    small[0].wait()
    small[1].wait()
    qf[0] = q_ref[:, :HD].astype(F32)
    qf[1] = q_ref[:, HD:].astype(F32)
    nf[0] = new_ref[:, 0, :].astype(F32)
    nf[1] = new_ref[:, 1, :].astype(F32)
    step_rows = [pl.ds(r, STEPS, stride=SLOTS + 1) for r in range(SLOTS + 1)]

    def own_rows(r):
        return (
            jnp.concatenate([qf[0, step_rows[r], :], qf[1, step_rows[r], :]], axis=0),
            nf[0, step_rows[r], :],
            nf[1, step_rows[r], :],
        )

    msg[...] = jnp.concatenate(own_rows(SLOTS), axis=0).astype(BF)
    own = [own_rows(r) for r in range(SLOTS)]
    keys_new = jnp.concatenate([k for _, k, _ in own], axis=0).astype(BF)
    values_new = jnp.concatenate([v for _, _, v in own], axis=0).astype(BF)

    for copy in small[2:] + kv_copies:
        copy.wait()

    lane16 = lax.broadcasted_iota(jnp.int32, (8, 16), 1)
    row16 = lax.broadcasted_iota(jnp.int32, (8, 16), 0) % STEPS
    context = []
    for r in range(SLOTS):
        blocks = [table[0, r * MAXB + j] for j in range(MAXB)]
        rows = attend(
            own[r][0].astype(BF),
            jnp.concatenate([kv[0, block] for block in blocks], axis=0),
            jnp.concatenate([kv[1, block] for block in blocks], axis=0),
            lengths[r, g],
            keys_new,
            values_new,
            (lane16 // STEPS == r) & (lane16 % STEPS <= row16),
        )
        context.append(jnp.concatenate([rows[:STEPS], rows[STEPS:]], axis=1))
    context = jnp.concatenate(context, axis=0).astype(BF)

    pl.semaphore_wait(barrier, len(peers))

    ask = remote(msg, asked, move_sem.at[0], move_sem.at[1], {"group": source, "mp": m})
    ask.start()
    theirs = pl.ds(pl.multiple_of((1 - zl) * (PAIR - WIN), 128), WIN)
    ours = pl.ds(pl.multiple_of(zl * (PAIR - WIN), 128), WIN)

    def z_copy(i):
        return remote(part.at[i, :, theirs], zrecv.at[i], zs.at[i], zr.at[i], other_peer(YS - 1))

    def project(i):
        w_copy(i).wait()
        part[i] = jnp.dot(context, w[i], preferred_element_type=F32).astype(BF)
        z_copy(i).start()

    each(YS, project)

    my_slot = mig_slot[g]
    my_hand = handover[g]
    row4 = lax.broadcasted_iota(jnp.int32, (STEPS, 1), 0)

    def of_slot(parts):
        rows = parts[0]
        for r in range(1, SLOTS):
            rows = jnp.where(my_slot == r, parts[r], rows)
        return rows

    none = jnp.zeros((16 - STEPS, HD), F32)
    keys_own = of_slot([k for _, k, _ in own])
    values_own = of_slot([v for _, _, v in own])
    blocks = [table[0, my_slot * MAXB + j] for j in range(MAXB)]
    ask.wait_recv()
    arrived = asked[...].astype(F32)
    rows = attend(
        arrived[:8].astype(BF),
        jnp.concatenate([kv[0, block] for block in blocks], axis=0),
        jnp.concatenate([kv[1, block] for block in blocks], axis=0),
        lengths[my_slot, g],
        jnp.concatenate([jnp.where(row4 >= my_hand, arrived[8:12], keys_own), none], axis=0).astype(BF),
        jnp.concatenate([jnp.where(row4 >= my_hand, arrived[12:], values_own), none], axis=0).astype(BF),
        lane16 <= row16,
    )
    rows = jnp.concatenate([rows[:STEPS], rows[STEPS:]], axis=1)
    ctx_out[...] = jnp.concatenate([rows] * 4, axis=0).astype(BF)
    give = remote(ctx_out, ctx_in, move_sem.at[2], move_sem.at[3], {"group": target, "mp": m})
    give.start()

    def y_copy(i):
        return remote(ysend.at[i], yrecv.at[i], ysem.at[i], yr.at[i], same_peer(i))

    def both(i):
        z_copy(i).wait_recv()
        return part[i, :, ours].astype(F32) + zrecv[i].astype(F32)

    def pair_sum(i):
        ysend[i] = both(i).astype(BF)
        y_copy(i).start()

    each(YS - 1, pair_sum)

    give.wait_recv()
    rows = ctx_in[...]
    tile_of = lax.broadcasted_iota(jnp.int32, (16, 128), 0) // STEPS

    def packed(product, first):
        tiles = [product[:, (first + c) * 128 : (first + c + 1) * 128] for c in range(4)]
        result = tiles[0]
        for c in range(1, 4):
            result = jnp.where(tile_of == c, tiles[c], result)
        return result

    def m_copy(i, k):
        n = 2 * i + k
        return remote(
            msend.at[n], mrecv.at[n], ms.at[n], mr.at[n], same_peer(i) if k else other_peer(i)
        )

    def project_two(p, same):
        products = [jnp.dot(rows, w[2 * p + k], preferred_element_type=F32) for k in range(2)]
        for k, product in enumerate(products):
            i = 2 * p + k
            low, high = packed(product, 0), packed(product, 3)
            same = jnp.where(zl == 0, low, high)
            msend[2 * i] = jnp.where(zl == 0, high, low).astype(BF)
            m_copy(i, 0).start()
            msend[2 * i + 1] = same.astype(BF)
            if k == 0:
                m_copy(i, 1).start()
            else:
                pl.when(p < YS // 2 - 1)(lambda: m_copy(i, 1).start())
        return same

    same = lax.fori_loop(0, YS // 2, project_two, jnp.zeros((16, 128), F32))

    def add_y(i, total):
        y_copy(i).wait_recv()
        return total + yrecv[i].astype(F32)

    total = lax.fori_loop(0, YS - 1, add_y, both(YS - 1))
    total = jnp.where(zl == 0, total, pltpu.roll(total, PAIR // 2, 1))
    for c in range(4):
        for r in range(SLOTS):
            moved = jnp.where(my_slot == r, my_hand, STEPS)
            stayed = total[4 * r : 4 * r + 4, c * 128 : c * 128 + 128]
            outf[c, step_rows[r], :] = jnp.where(row4 >= moved, 0.0, stayed)

    ask.wait_send()
    give.wait_send()

    def sent(i):
        z_copy(i).wait_send()
        y_copy(i).wait_send()
        m_copy(i, 0).wait_send()
        m_copy(i, 1).wait_send()

    each(YS - 1, sent)
    z_copy(YS - 1).wait_send()
    m_copy(YS - 1, 0).wait_send()

    def add_m(i, total):
        m_copy(i, 0).wait_recv()
        m_copy(i, 1).wait_recv()
        return total + mrecv[2 * i].astype(F32) + mrecv[2 * i + 1].astype(F32)

    same = lax.fori_loop(0, YS - 1, add_m, same)
    m_copy(YS - 1, 0).wait_recv()
    same = same + mrecv[2 * YS - 2].astype(F32)
    same = jnp.concatenate([same[4 * c : 4 * c + 4] for c in range(4)], axis=1)
    same = jnp.where(zl == 0, same, pltpu.roll(same, PAIR // 2, 1))
    for c in range(4):
        outf[c, step_rows[SLOTS], :] = jnp.where(
            row4 >= handover[source], same[:, c * 128 : c * 128 + 128], 0.0
        )
    wide = jnp.concatenate([outf[c] for c in range(4)], axis=1)
    out_ref[...] = wide[:, : PAIR // 2].astype(BF)


def on_device(
    queries, new_kv, kv_pool, block_table, lengths, mig_slot, mig_hop, handover, out_weight
):
    rows = STEPS * (SLOTS + 1)
    width = out_weight.shape[1]
    new_kv = new_kv.transpose(1, 0, 2)
    lengths = lengths.T
    vmem = pl.BlockSpec(memory_space=pltpu.VMEM)
    hbm = pl.BlockSpec(memory_space=pltpu.HBM)
    dma = lambda n: pltpu.SemaphoreType.DMA((n,))
    tile = (16, 128)
    call = lambda hop: pl.pallas_call(
        functools.partial(kernel, hop),
        out_shape=jax.ShapeDtypeStruct((rows, PAIR // 2), BF),
        in_specs=[hbm] * 8,
        out_specs=vmem,
        scratch_shapes=[
            pltpu.SMEM(block_table.shape, jnp.int32),
            pltpu.SMEM(lengths.shape, jnp.int32),
            pltpu.SMEM(mig_slot.shape, jnp.int32),
            pltpu.SMEM(handover.shape, jnp.int32),
            pltpu.VMEM(queries.shape, BF),
            pltpu.VMEM(new_kv.shape, BF),
            pltpu.VMEM((2, rows, HD), F32),
            pltpu.VMEM((2, rows, HD), F32),
            pltpu.VMEM(kv_pool.shape, BF),
            pltpu.VMEM((YS, 2 * HD, PAIR), BF),
            pltpu.VMEM((YS, 16, PAIR), BF),
            pltpu.VMEM((YS, 16, WIN), BF),
            pltpu.VMEM((YS, 16, WIN), BF),
            pltpu.VMEM((YS, 16, WIN), BF),
            pltpu.VMEM(tile, BF),
            pltpu.VMEM(tile, BF),
            pltpu.VMEM((16, 2 * HD), BF),
            pltpu.VMEM((16, 2 * HD), BF),
            pltpu.VMEM((2 * YS,) + tile, BF),
            pltpu.VMEM((2 * YS,) + tile, BF),
            pltpu.VMEM((4, rows, 128), F32),
            dma(6), dma(2), dma(YS), dma(YS), dma(YS), dma(YS), dma(YS), dma(2 * YS), dma(2 * YS), dma(4),
        ],
        compiler_params=pltpu.CompilerParams(
            collective_id=hop, has_side_effects=True, vmem_limit_bytes=60 * 1024 * 1024
        ),
        cost_estimate=pl.CostEstimate(
            flops=2 * 16 * 256 * width, bytes_accessed=5 * 1024 * 1024, transcendentals=32 * 512
        ),
    )
    return lax.switch(
        mig_hop[0] - 1, [call(hop) for hop in range(1, GROUPS)],
        block_table, lengths, mig_slot, handover, queries, new_kv, kv_pool, out_weight,
    )


def solution(mesh):
    in_specs = (
        P("group", "mp"),
        P(None, "group", "mp"),
        P(None, "group", None, "mp"),
        P("group", None),
        P(),
        P(),
        P(),
        P(),
        P("mp", None),
    )
    return jax.shard_map(
        on_device, mesh=mesh, in_specs=in_specs, out_specs=P("group", "mp"), check_vma=False
    )
```
